768 devices in a mesh: ta: 16 (over y_lo, x, core), sa: 48 (over z, y_hi).
Axes of the slice: x: 4, y: 8 (y_hi: 4, y_lo: 2; y = y_hi * 2 + y_lo), z: 12, core: 2. Of those that a mesh axis runs over, the one named last changes fastest.
Arguments:
- operator: bfloat16 [32, 96, 6, 82944], P('ta', 'sa'), may hold values from -0.625 to 0.625
- vectors: bfloat16 [32, 96, 6, 6144], P('ta', 'sa'), may hold values from -2.5 to 2.5
- aggregate: int32 [6], replicated, may hold values from 0 to 1, as said below
Outputs:
- within_cell: float32 [16, 48, 3, 2, 2, 4096], P('ta', 'sa')
- cross_links: float32 [16, 48, 4, 2, 4096], P('ta', 'sa')
The draws below stay inside these ranges and needn't reach their ends.
Inputs may be any that keep to these rules, and one draw needn't show every extreme that they name: Every aggregate number is taken by exactly 2 * 3 / 2 sites.
All inputs are finite; a program needn't handle non-finite values.
Results may differ from the reference program's by a relative error of at most 0.0029.
Values may be sent and summed in bfloat16 or wider, within the bound.
A program may use at most 64 MiB of HBM per device.

```python
import jax
import jax.numpy as jnp
import numpy as np
from jax import lax

BLOCK = 96
NULLCOLS = 64
LX = 2
LY = 3
XSPLIT = 8
ZDEV = 2
AGGS = 2
NT = 32
N_SA = 48


def draw_aggregate(key, part):
    shuffled = jax.random.permutation(key, LX * LY)
    return (shuffled // (LX * LY // AGGS)).astype(jnp.int32)


def block_levels(own_key, extent, shards, smallest, largest):
    def one(position, blocks):
        heights = jax.random.uniform(jax.random.fold_in(jax.random.fold_in(own_key, 6), position), (blocks,), jnp.float32, smallest / len(shards), largest / len(shards))
        return jnp.repeat(jnp.exp(heights), extent[position] // blocks).reshape((-1,) + (1,) * (len(extent) - position - 1))

    loudness = one(*shards[0])
    for cut in shards[1:]:
        loudness = loudness * one(*cut)
    return loudness


def gaussian(rng, shape, scale, reach, shards=(), held_as=jnp.bfloat16):
    drawn = scale * jax.random.normal(rng, shape, jnp.float32)
    if shards:
        drawn = drawn * block_levels(rng, shape, shards, -0.22, 0.18)
    return jnp.clip(drawn, -reach, reach).astype(held_as)


def setup_inputs(seed: int = 0) -> dict:
    arg_keys = jax.random.split(jax.random.key(seed), 4)
    return {
        "operator": gaussian(arg_keys[0], (NT, N_SA * ZDEV, LX * LY, 9 * BLOCK * BLOCK), BLOCK ** -0.5, 0.625, ((0, 16), (1, 48))),
        "vectors": gaussian(arg_keys[1], (NT, N_SA * ZDEV, LX * LY, BLOCK * NULLCOLS), 0.25, 2.5, ((0, 16), (1, 48))),
        "aggregate": draw_aggregate(jax.random.fold_in(arg_keys[3], 71), 0),
    }


PRECISE = lax.Precision.HIGHEST


def neighbour_table():
    places = np.arange(LX * LY)
    first_coord = places // LY
    second_coord = places % LY
    plus_first = ((first_coord + 1) % LX) * LY + second_coord
    minus_first = ((first_coord - 1) % LX) * LY + second_coord
    plus_second = first_coord * LY + (second_coord + 1) % LY
    minus_second = first_coord * LY + (second_coord - 1) % LY
    return np.stack([places, places, places, places, places, plus_first, minus_first, plus_second, minus_second])


def natural(plane):
    z_slabs = N_SA // XSPLIT
    field = plane.reshape(z_slabs, XSPLIT, ZDEV, LX, LY, plane.shape[-1])
    field = field.transpose(0, 2, 1, 3, 4, 5)
    return field.reshape(z_slabs * ZDEV, XSPLIT * LX, LY, plane.shape[-1])


def plane_contrib(operator, vectors, aggregate, plane_index):
    time_count = vectors.shape[0]
    current = natural(lax.dynamic_index_in_dim(vectors, plane_index, 0, keepdims=False))
    forward_plane = natural(lax.dynamic_index_in_dim(vectors, (plane_index + 1) % time_count, 0, keepdims=False))
    behind = natural(lax.dynamic_index_in_dim(vectors, (plane_index + time_count - 1) % time_count, 0, keepdims=False))
    matrices = natural(lax.dynamic_index_in_dim(operator, plane_index, 0, keepdims=False))
    z_count = current.shape[0]
    x_count = current.shape[1]

    def as_blocks(field):
        return field.reshape(z_count, x_count, LY, BLOCK, NULLCOLS).astype(jnp.float32)

    beside = jnp.stack([as_blocks(current), as_blocks(forward_plane), as_blocks(behind),
                        as_blocks(jnp.roll(current, -1, 0)), as_blocks(jnp.roll(current, 1, 0)),
                        as_blocks(jnp.roll(current, -1, 1)), as_blocks(jnp.roll(current, 1, 1)),
                        as_blocks(jnp.roll(current, -1, 2)), as_blocks(jnp.roll(current, 1, 2))], axis=3)
    weights = matrices.reshape(z_count, x_count, LY, 9, BLOCK, BLOCK).astype(jnp.float32)
    images = jnp.einsum("zxymij,zxymjk->zxymik", weights, beside, precision=PRECISE).astype(jnp.bfloat16)
    images = lax.optimization_barrier(images).astype(jnp.float32)
    contrib = jnp.einsum("zxyji,zxymjk->zxymik", beside[:, :, :, 0], images, precision=PRECISE)
    local_sites = (np.arange(x_count) % LX)[:, None] * LY + np.arange(LY)[None, :]
    member_all = (aggregate[:, None] == jnp.arange(AGGS, dtype=jnp.int32)[None, :]).astype(jnp.float32)
    member = member_all[local_sites]
    target = member_all[neighbour_table()[:, local_sites]]
    even_time = (plane_index % 2 == 0).astype(jnp.float32)
    odd_space = (jnp.arange(z_count, dtype=jnp.int32) % 2).astype(jnp.float32)
    filled_z = jnp.ones((z_count,), jnp.float32)
    cross_mask = jnp.stack([even_time * filled_z, (1.0 - even_time) * filled_z, 1.0 - odd_space, odd_space], axis=1)
    x_local = jnp.arange(x_count, dtype=jnp.int32) % LX
    x_last = jnp.broadcast_to((x_local == LX - 1).astype(jnp.float32)[None, :], (z_count, x_count))
    x_first = jnp.broadcast_to((x_local == 0).astype(jnp.float32)[None, :], (z_count, x_count))
    filled = jnp.ones((z_count, x_count), jnp.float32)
    blank = jnp.zeros((z_count, x_count), jnp.float32)
    columns = [jnp.broadcast_to(cross_mask[:, k][:, None], (z_count, x_count)) for k in range(4)]
    route_same = jnp.stack([filled, 1.0 - columns[0], 1.0 - columns[1], 1.0 - columns[2], 1.0 - columns[3],
                            1.0 - x_last, 1.0 - x_first, filled, filled], axis=2)
    route_next = jnp.stack([blank, blank, blank, blank, blank, x_last, blank, blank, blank], axis=2)
    route_prior = jnp.stack([blank, blank, blank, blank, blank, blank, x_first, blank, blank], axis=2)
    route = jnp.stack([route_same, route_next, route_prior], axis=0)
    within = jnp.einsum("zxymik,xya,rzxm,mxyb->zxrabik", contrib, member, route, target, precision=PRECISE)
    crossing = jnp.einsum("zxykij,zk,xya->zxkaij", contrib[:, :, :, 1:5], cross_mask, member, precision=PRECISE)
    coarse = jnp.concatenate([within.reshape(z_count, x_count, 3 * AGGS, AGGS, NULLCOLS * NULLCOLS),
                              crossing.reshape(z_count, x_count, 4, AGGS, NULLCOLS * NULLCOLS)], axis=2)
    coarse = coarse.reshape((z_count, x_count // LX, LX) + coarse.shape[2:]).sum(axis=2)
    rolled = jnp.roll(coarse, 1, 0)
    return rolled.reshape((z_count // 2, 2) + rolled.shape[1:]).sum(axis=1)


def reference(operator, vectors, aggregate):
    time_count = vectors.shape[0]
    per_plane = lax.map(lambda plane_index: plane_contrib(operator, vectors, aggregate, plane_index),
                        jnp.arange(time_count, dtype=jnp.int32))
    rolled = jnp.roll(per_plane, 1, 0)
    coarse = rolled.reshape((time_count // 2, 2) + rolled.shape[1:]).sum(axis=1)
    paired = ZDEV // 2
    z_slabs = N_SA // XSPLIT
    ordered = coarse.reshape((time_count // 2, z_slabs, paired, XSPLIT) + coarse.shape[3:])
    ordered = ordered.transpose(0, 1, 3, 2, 4, 5, 6)
    ordered = ordered.reshape((time_count // 2, N_SA * paired) + coarse.shape[3:])
    within_cell = ordered[:, :, :3 * AGGS].reshape(time_count // 2, N_SA * paired, 3, AGGS, AGGS,
                                                   NULLCOLS * NULLCOLS)
    return within_cell, ordered[:, :, 3 * AGGS:]
```

```python
import jax
import jax.numpy as jnp
from jax import lax
from jax.experimental import pallas as pl
from jax.experimental.pallas import tpu as pltpu
from jax.sharding import PartitionSpec as P

BLOCK = 96
NULLCOLS = 64
LX = 2
LY = 3
XSPLIT = 8
AGGS = 2
SITES = LX * LY
HOPS = 9
LANES = 128
GROUPS = BLOCK // 4
MESH = pl.DeviceIdType.MESH
F32 = jnp.float32
BF16 = jnp.bfloat16


def lane_half(rows):
    return lax.broadcasted_iota(jnp.int32, (rows, LANES), 1) < NULLCOLS


def swap(value):
    return pltpu.roll(value, NULLCOLS, 1)


def block_weights(packed):
    low = lane_half(BLOCK)
    wide = packed.astype(F32)
    turned = swap(wide)
    zero = jnp.zeros_like(wide)
    gap = jnp.zeros((2 * LANES - 2 * BLOCK, LANES), BF16)
    out = []
    for first, second in ((wide, turned), (turned, wide)):
        left = jnp.where(low, first, zero).astype(BF16)
        right = jnp.where(low, zero, second).astype(BF16)
        out.append((jnp.concatenate([left, right, gap], axis=0), jnp.concatenate([gap, left, right], axis=0)))
    return out


def kernel(
    agg_ref, op_hbm, vec_hbm, within_ref, cross_ref,
    op_v, vec_v, op_f, vec_f, mix, pack_z, pack_x, halo_t, halo_z, halo_x, img, turn, left, rhs,
    part, pt_out, pt_in, pz_out, pz_in, load_sem, send_sem, recv_sem,
):
    nt = lax.axis_size("ta")
    ns = lax.axis_size("sa")
    ti = lax.axis_index("ta")
    sj = lax.axis_index("sa")
    slab = sj // XSPLIT * XSPLIT
    xi = sj % XSPLIT
    t_up = ((ti + 1) % nt, sj)
    t_down = ((ti + nt - 1) % nt, sj)
    z_up = (ti, (sj + XSPLIT) % ns)
    z_down = (ti, (sj + ns - XSPLIT) % ns)
    x_up = (ti, slab + (xi + 1) % XSPLIT)
    x_down = (ti, slab + (xi + XSPLIT - 1) % XSPLIT)

    barrier = pltpu.get_barrier_semaphore()
    for there in (t_up, t_down, z_up, z_down, x_up, x_down):
        pl.semaphore_signal(barrier, inc=1, device_id=there, device_id_type=MESH)
    vec_load = pltpu.make_async_copy(vec_hbm, vec_v, load_sem.at[2])
    vec_load.start()
    op_loads = [pltpu.make_async_copy(op_hbm.at[t], op_v.at[t], load_sem.at[t]) for t in range(2)]
    for load in op_loads:
        load.start()

    def remote(index, src, dst, there):
        return pltpu.make_async_remote_copy(
            src_ref=src, dst_ref=dst, send_sem=send_sem.at[index], recv_sem=recv_sem.at[index],
            device_id=there, device_id_type=MESH,
        )

    vec_load.wait()
    low48 = lane_half(48)

    def vec_site(ts, carry):
        vec_f[ts] = vec_v[ts // SITES, ts % SITES].astype(F32)
        v0 = vec_f[ts, pl.ds(0, 48, stride=2), :]
        v1 = vec_f[ts, pl.ds(1, 48, stride=2), :]
        mix[0, pl.ds(0, 48, stride=2), :] = jnp.where(low48, v0, swap(v1))
        mix[0, pl.ds(1, 48, stride=2), :] = jnp.where(low48, swap(v0), v1)
        pack_z[ts // SITES, ts % SITES] = mix[0].astype(BF16)
        return carry

    lax.fori_loop(0, 2 * SITES, vec_site, 0)

    def vec_pair(tzx, carry):
        t, z, x2 = tzx // 6, tzx // 3 % 2, tzx % 3
        v0 = vec_f[t * SITES + x2, pl.ds(z, 48, stride=2), :]
        v1 = vec_f[t * SITES + LY + x2, pl.ds(z, 48, stride=2), :]
        mix[1, pl.ds(0, 48, stride=2), :] = jnp.where(low48, v0, swap(v1))
        mix[1, pl.ds(1, 48, stride=2), :] = jnp.where(low48, swap(v0), v1)
        pack_x[t, z, x2] = mix[1].astype(BF16)
        return carry

    lax.fori_loop(0, 12, vec_pair, 0)

    pl.semaphore_wait(barrier, 6)
    t_face = {
        1: remote(0, pack_x.at[1], halo_t.at[0], t_up),
        0: remote(1, pack_x.at[0], halo_t.at[1], t_down),
    }
    t_face[1].start()
    t_face[0].start()
    faces = {}
    for t in (1, 0):
        faces[t] = (
            remote(2 + 4 * t, pack_z.at[t, LY:SITES], halo_x.at[0, t], x_up),
            remote(3 + 4 * t, pack_z.at[t, 0:LY], halo_x.at[1, t], x_down),
            remote(4 + 4 * t, pack_x.at[t, 1], halo_z.at[0, t], z_up),
            remote(5 + 4 * t, pack_x.at[t, 0], halo_z.at[1, t], z_down),
        )
        for face in faces[t]:
            face.start()

    for t in range(2):
        op_loads[t].wait()

        def widen(s, carry):
            op_f[t * SITES + s] = op_v[t, s].astype(F32)
            return carry

        lax.fori_loop(0, SITES, widen, 0)

    def rows_of(ts, z, hop):
        return [
            op_f[ts, pl.ds(hop * 144 + 2 * v + z, GROUPS, stride=6), :] for v in range(3)
        ]

    def images(users, weights):
        parts = [rows_of(ts, z, hop) for ts, z, hop in users]
        tiles = [jnp.concatenate([part[v] for part in parts], axis=0).astype(BF16) for v in range(3)]
        for half in range(2):
            got = jnp.dot(
                jnp.concatenate([tiles[half], tiles[half + 1]], axis=1), weights[half],
                preferred_element_type=F32,
            ).astype(BF16).astype(F32)
            for i, (ts, z, hop) in enumerate(users):
                img[ts * 2 + z, hop, :, LANES * half:LANES * (half + 1)] = got[GROUPS * i:GROUPS * (i + 1)]

    def local(tz, carry):
        t, z = tz // 2, tz % 2
        for x2 in range(LY):
            both = block_weights(pack_x[t, z, x2])
            for x1 in range(LX):
                s = x1 * LY + x2
                users = (
                    (t * SITES + s, z, 0),
                    ((1 - t) * SITES + s, z, 2 - t),
                    (t * SITES + s, 1 - z, 4 - z),
                    (t * SITES + (1 - x1) * LY + x2, z, 5 if x1 == 1 else 6),
                    (t * SITES + x1 * LY + (x2 + 2) % LY, z, 7),
                    (t * SITES + x1 * LY + (x2 + 1) % LY, z, 8),
                )
                images(users, both[x1])
        return carry

    lax.fori_loop(0, 4, local, 0)

    column = lax.broadcasted_iota(jnp.int32, (1, SITES * GROUPS), 1)
    member = [agg_ref[s].astype(F32) for s in range(SITES)]
    others = [1.0 - m for m in member]
    weight_of = (others, member)
    mask = []
    for a in range(AGGS):
        row = jnp.zeros((1, SITES * GROUPS), F32)
        for s in range(SITES):
            inside = jnp.logical_and(column >= s * GROUPS, column < (s + 1) * GROUPS)
            row = row + jnp.where(inside, weight_of[a][s], 0.0)
        mask.append(row)
    pad = jnp.zeros((2 * LANES - SITES * GROUPS, LANES), F32)

    def left_side(tz, carry):
        t, z = tz // 2, tz % 2
        for h in range(2):
            blocks = [vec_f[t * SITES + s, pl.ds(2 * h + z, GROUPS, stride=4), :] for s in range(SITES)]
            turned = jnp.transpose(jnp.concatenate(blocks + [pad], axis=0))
            for side in range(2):
                turn[side] = turned[:, LANES * side:LANES * (side + 1)]
            for low in range(2):
                for par in range(2):
                    rows = jnp.concatenate(
                        [turn[side, pl.ds(low * NULLCOLS + par, 32, stride=2), :] for side in range(2)], axis=1
                    )[:, :SITES * GROUPS]
                    for a in range(AGGS):
                        at = ((a * 2 + low) * 2 + par) * 32
                        left[tz, h, at:at + 32, :] = (rows * mask[a]).astype(BF16)
        return carry

    lax.fori_loop(0, 4, left_side, 0)

    def halo(t):
        def below_above(zx, carry):
            z, x2 = zx // LY, zx % LY
            both = block_weights(halo_t[t, z, x2])
            for x1 in range(LX):
                images(((t * SITES + x1 * LY + x2, z, 2 - t),), both[x1])
            return carry

        def z_side(zx, carry):
            z, x2 = zx // LY, zx % LY
            both = block_weights(halo_z[z, t, x2])
            for x1 in range(LX):
                images(((t * SITES + x1 * LY + x2, z, 4 - z),), both[x1])
            return carry

        def x_side(s, carry):
            x1, x2 = s // LY, s % LY
            both = block_weights(halo_x[x1, t, x2])
            for z in range(2):
                images(((t * SITES + s, z, 6 - x1),), both[z])
            return carry

        return below_above, z_side, x_side

    low32 = lane_half(32)

    def quarter(t, z, keep):
        tz = t * 2 + z
        t_stay, t_leave = (1, 2) if t == 1 else (2, 1)
        z_stay, z_leave = (3, 4) if z == 1 else (4, 3)
        for h in range(2):
            cut = slice(LANES * h, LANES * (h + 1))
            columns = [[] for _ in range(8)]
            blank = jnp.zeros((GROUPS, LANES), F32)
            for s in range(SITES):
                x1, x2 = s // LY, s % LY
                at = (t * SITES + s) * 2 + z
                take = lambda hop: img[at, hop, :, cut]
                same = take(0) + take(t_stay) + take(z_stay)
                x_stay, x_leave = (6, 5) if x1 == 1 else (5, 6)
                across = (1 - x1) * LY + x2
                up, down = x1 * LY + (x2 + 1) % LY, x1 * LY + (x2 + 2) % LY
                inner, plus, minus, outer = take(x_stay), take(7), take(8), take(x_leave)
                for b in range(AGGS):
                    w = weight_of[b]
                    columns[b].append(w[s] * same + w[across] * inner + w[up] * plus + w[down] * minus)
                    columns[2 + b].append(w[across] * outer if x1 == 1 else blank)
                    columns[4 + b].append(w[across] * outer if x1 == 0 else blank)
                columns[6].append(take(t_leave))
                columns[7].append(take(z_leave))
            for n in range(4):
                rhs[h, n] = jnp.concatenate(
                    [jnp.concatenate(columns[2 * n + c], axis=0).astype(BF16) for c in range(2)], axis=1
                )
        for n in range(4):
            for a in range(AGGS):
                rows = slice(LANES * a, LANES * (a + 1))
                got = jnp.dot(left[tz, 0, rows, :], rhs[0, n], preferred_element_type=F32)
                got = got + jnp.dot(left[tz, 1, rows, :], rhs[1, n], preferred_element_type=F32)
                for c in range(2):
                    cut = got[:, LANES * c:LANES * (c + 1)]
                    value = jnp.where(
                        low32, cut[0:32] + swap(cut[64:96]), swap(cut[32:64]) + cut[96:128]
                    )
                    keep(n * 4 + a * 2 + c if n < 3 else 12 + c * 2 + a, value)

    def send_block(z):
        def keep(block, value):
            pt_out[z, block] = value.astype(BF16)

        return keep

    def keep_block(z):
        def keep(block, value):
            part[z, block] = value

        return keep

    def halo_done(t):
        below_above, z_side, x_side = halo(t)
        t_face[1 - t].wait_recv()
        lax.fori_loop(0, 6, below_above, 0)
        faces[t][0].wait_recv()
        faces[t][1].wait_recv()
        lax.fori_loop(0, 6, x_side, 0)
        faces[t][2].wait_recv()
        faces[t][3].wait_recv()
        lax.fori_loop(0, 6, z_side, 0)

    pt = {z: remote(10 + z, pt_out.at[z], pt_in.at[z], t_up) for z in range(2)}
    pz = remote(12, pz_out, pz_in, z_up)

    halo_done(1)
    quarter(1, 1, send_block(1))
    pt[1].start()
    quarter(1, 0, send_block(0))
    pt[0].start()
    halo_done(0)
    quarter(0, 1, keep_block(1))
    pt[1].wait_recv()
    for block in range(12):
        pz_out[block] = (part[1, block] + pt_in[1, block].astype(F32)).astype(BF16)
    for a in range(AGGS):
        pz_out[12 + a] = part[1, 12 + a].astype(BF16)
        pz_out[14 + a] = pt_in[1, 12 + a]
        pz_out[16 + a] = (part[1, 14 + a] + pt_in[1, 14 + a].astype(F32)).astype(BF16)
    pz.start()
    quarter(0, 0, keep_block(0))
    pt[0].wait_recv()
    for block in range(12):
        part[0, block] = part[0, block] + pt_in[0, block].astype(F32)
    for a in range(AGGS):
        part[0, 14 + a] = part[0, 14 + a] + pt_in[0, 14 + a].astype(F32)
    pz.wait_recv()
    for block in range(12):
        ra, b = block // 2, block % 2
        within_ref[ra, pl.ds(b, 32, stride=2), :] = part[0, block] + pz_in[block].astype(F32)
    for a in range(AGGS):
        cross_ref[0, pl.ds(a, 32, stride=2), :] = part[0, 12 + a] + pz_in[12 + a].astype(F32)
        cross_ref[1, pl.ds(a, 32, stride=2), :] = pt_in[0, 12 + a].astype(F32) + pz_in[14 + a].astype(F32)
        cross_ref[2, pl.ds(a, 32, stride=2), :] = part[0, 14 + a]
        cross_ref[3, pl.ds(a, 32, stride=2), :] = pz_in[16 + a].astype(F32)
    for copy in (t_face[0], t_face[1], *faces[0], *faces[1], pt[0], pt[1], pz):
        copy.wait_send()


def lane_tiles(field):
    time, depth, sites, length = field.shape
    split = field.reshape(time, depth, sites, length // LANES, LANES)
    return split.transpose(0, 2, 3, 1, 4).reshape(time, sites, length // LANES * depth, LANES)


def per_device(operator, vectors, aggregate):
    op_rows = HOPS * BLOCK * BLOCK // LANES * 2
    vec_rows = BLOCK * NULLCOLS // LANES * 2
    within, cross = pl.pallas_call(
        kernel,
        out_shape=(
            jax.ShapeDtypeStruct((3 * AGGS, 64, LANES), F32),
            jax.ShapeDtypeStruct((4, 64, LANES), F32),
        ),
        in_specs=[
            pl.BlockSpec(memory_space=pltpu.SMEM),
            pl.BlockSpec(memory_space=pltpu.HBM),
            pl.BlockSpec(memory_space=pltpu.HBM),
        ],
        out_specs=[pl.BlockSpec(memory_space=pltpu.VMEM)] * 2,
        scratch_shapes=[
            pltpu.VMEM((2, SITES, op_rows, LANES), BF16),
            pltpu.VMEM((2, SITES, vec_rows, LANES), BF16),
            pltpu.VMEM((2 * SITES, op_rows, LANES), F32),
            pltpu.VMEM((2 * SITES, vec_rows, LANES), F32),
            pltpu.VMEM((2, BLOCK, LANES), F32),
            pltpu.VMEM((2, SITES, BLOCK, LANES), BF16),
            pltpu.VMEM((2, 2, LY, BLOCK, LANES), BF16),
            pltpu.VMEM((2, 2, LY, BLOCK, LANES), BF16),
            pltpu.VMEM((2, 2, LY, BLOCK, LANES), BF16),
            pltpu.VMEM((2, 2, LY, BLOCK, LANES), BF16),
            pltpu.VMEM((4 * SITES, HOPS, GROUPS, 2 * LANES), F32),
            pltpu.VMEM((2, LANES, LANES), F32),
            pltpu.VMEM((4, 2, 2 * LANES, SITES * GROUPS), BF16),
            pltpu.VMEM((2, 4, SITES * GROUPS, 2 * LANES), BF16),
            pltpu.VMEM((2, 16, 32, LANES), F32),
            pltpu.VMEM((2, 16, 32, LANES), BF16),
            pltpu.VMEM((2, 16, 32, LANES), BF16),
            pltpu.VMEM((18, 32, LANES), BF16),
            pltpu.VMEM((18, 32, LANES), BF16),
            pltpu.SemaphoreType.DMA((3,)),
            pltpu.SemaphoreType.DMA((13,)),
            pltpu.SemaphoreType.DMA((13,)),
        ],
        compiler_params=pltpu.CompilerParams(
            collective_id=0, has_side_effects=True, vmem_limit_bytes=60 << 20
        ),
    )(aggregate, lane_tiles(operator), lane_tiles(vectors))
    within = within.reshape(3, AGGS, 32, AGGS, LANES).transpose(0, 1, 3, 2, 4)
    cross = cross.reshape(4, 32, AGGS, LANES).transpose(0, 2, 1, 3)
    return (
        within.reshape(1, 1, 3, AGGS, AGGS, NULLCOLS * NULLCOLS),
        cross.reshape(1, 1, 4, AGGS, NULLCOLS * NULLCOLS),
    )


def solution(mesh):
    return jax.shard_map(
        per_device,
        mesh=mesh,
        in_specs=(P("ta", "sa", None, None), P("ta", "sa", None, None), P()),
        out_specs=(P("ta", "sa", None, None, None, None), P("ta", "sa", None, None, None)),
        check_vma=False,
    )
```

```python
import jax
import jax.numpy as jnp
from jax import lax
from jax.experimental import pallas as pl
from jax.experimental.pallas import tpu as pltpu
from jax.sharding import PartitionSpec as P

BLOCK = 96
NULLCOLS = 64
LX = 2
LY = 3
XSPLIT = 8
AGGS = 2
SITES = LX * LY
HOPS = 9
LANES = 128
GROUPS = BLOCK // 4
MESH = pl.DeviceIdType.MESH
F32 = jnp.float32
BF16 = jnp.bfloat16


def lane_half(rows):
    return lax.broadcasted_iota(jnp.int32, (rows, LANES), 1) < NULLCOLS


def swap(value):
    return pltpu.roll(value, NULLCOLS, 1)


def block_weights(packed):
    low = lane_half(BLOCK)
    wide = packed.astype(F32)
    turned = swap(wide)
    zero = jnp.zeros_like(wide)
    gap = jnp.zeros((2 * LANES - 2 * BLOCK, LANES), BF16)
    out = []
    for first, second in ((wide, turned), (turned, wide)):
        left = jnp.where(low, first, zero).astype(BF16)
        right = jnp.where(low, zero, second).astype(BF16)
        out.append((jnp.concatenate([left, right, gap], axis=0), jnp.concatenate([gap, left, right], axis=0)))
    return out


def kernel(
    agg_hbm, op_hbm, vec_hbm, within_ref, cross_ref,
    agg_ref, op_v, vec_v, op_f, vec_f, mix, pack_t, pack_x, halo_t, halo_z, halo_x, img, turn, left,
    part, pt_out, pt_in, pz_out, pz_in, load_sem, send_sem, recv_sem,
):
    nt = lax.axis_size("ta")
    ns = lax.axis_size("sa")
    ti = lax.axis_index("ta")
    sj = lax.axis_index("sa")
    slab = sj // XSPLIT * XSPLIT
    xi = sj % XSPLIT
    t_up = ((ti + 1) % nt, sj)
    t_down = ((ti + nt - 1) % nt, sj)
    z_up = (ti, (sj + XSPLIT) % ns)
    z_down = (ti, (sj + ns - XSPLIT) % ns)
    x_up = (ti, slab + (xi + 1) % XSPLIT)
    x_down = (ti, slab + (xi + XSPLIT - 1) % XSPLIT)

    barrier = pltpu.get_barrier_semaphore()
    for there in (t_up, t_down, z_up, z_down, x_up, x_down):
        pl.semaphore_signal(barrier, inc=1, device_id=there, device_id_type=MESH)
    vec_load = pltpu.make_async_copy(vec_hbm, vec_v, load_sem.at[2])
    vec_load.start()
    agg_load = pltpu.make_async_copy(agg_hbm, agg_ref, load_sem.at[3])
    agg_load.start()
    op_loads = [pltpu.make_async_copy(op_hbm.at[t], op_v.at[t], load_sem.at[t]) for t in range(2)]
    for load in op_loads:
        load.start()

    def remote(index, src, dst, there):
        return pltpu.make_async_remote_copy(
            src_ref=src, dst_ref=dst, send_sem=send_sem.at[index], recv_sem=recv_sem.at[index],
            device_id=there, device_id_type=MESH,
        )

    vec_load.wait()
    low48 = lane_half(48)

    def vec_wide(ts, carry):
        vec_f[ts] = vec_v[ts // SITES, ts % SITES].astype(F32)
        return carry

    lax.fori_loop(0, 2 * SITES, vec_wide, 0, unroll=4)

    def paired(first, second, z, spare):
        v0 = vec_f[first, pl.ds(z, 48, stride=2), :]
        v1 = vec_f[second, pl.ds(z, 48, stride=2), :]
        mix[spare, pl.ds(0, 48, stride=2), :] = jnp.where(low48, v0, swap(v1))
        mix[spare, pl.ds(1, 48, stride=2), :] = jnp.where(low48, swap(v0), v1)
        return mix[spare].astype(BF16)

    def pair_times(z):
        def one(s, carry):
            pack_t[z, s] = paired(s, SITES + s, z, s % 4)
            return carry

        lax.fori_loop(0, SITES, one, 0, unroll=True)

    def pair_sites(z):
        def one(tx, carry):
            t, x2 = tx // LY, tx % LY
            pack_x[z, t, x2] = paired(t * SITES + x2, t * SITES + LY + x2, z, tx % 4)
            return carry

        lax.fori_loop(0, SITES, one, 0, unroll=True)

    x_face, t_face = {}, {}
    for z in range(2):
        x_face[z] = (
            remote(2 * z, pack_t.at[z, LY:SITES], halo_x.at[0, z], x_up),
            remote(2 * z + 1, pack_t.at[z, 0:LY], halo_x.at[1, z], x_down),
        )
        t_face[z] = (
            remote(4 + 2 * z, pack_x.at[z, 1], halo_t.at[0, z], t_up),
            remote(5 + 2 * z, pack_x.at[z, 0], halo_t.at[1, z], t_down),
        )
    z_face = (
        remote(8, pack_x.at[1], halo_z.at[0], z_up),
        remote(9, pack_x.at[0], halo_z.at[1], z_down),
    )
    cuts = (slice(0, 4), slice(4, 12), slice(12, 16))
    pt = {
        (1, c): remote(10 + c, pt_out.at[1, cuts[c]], pt_in.at[1, cuts[c]], t_up) for c in range(3)
    }
    pt[0, 0] = remote(13, pt_out.at[0, 0:4], pt_in.at[0, 0:4], t_up)
    pt[0, 1] = remote(14, pt_out.at[0, 4:16], pt_in.at[0, 4:16], t_up)
    pz_cuts = (slice(0, 4), slice(4, 12), slice(12, 18))
    pz = [remote(15 + c, pz_out.at[pz_cuts[c]], pz_in.at[pz_cuts[c]], z_up) for c in range(3)]

    pair_times(1)
    pl.semaphore_wait(barrier, 6)
    for face in x_face[1]:
        face.start()
    pair_sites(0)
    z_face[1].start()
    pair_sites(1)
    z_face[0].start()
    for face in t_face[1]:
        face.start()
    pair_times(0)
    for face in (*x_face[0], *t_face[0]):
        face.start()

    for t in (1, 0):
        op_loads[t].wait()

        def widen(s, carry):
            op_f[t * SITES + s] = op_v[t, s].astype(F32)
            return carry

        lax.fori_loop(0, SITES, widen, 0)

    def rows_of(ts, z, hop):
        return [
            op_f[ts, pl.ds(hop * 144 + 2 * v + z, GROUPS, stride=6), :] for v in range(3)
        ]

    def images(users, weights):
        parts = [rows_of(ts, z, hop) for ts, z, hop in users]
        tiles = [jnp.concatenate([part[v] for part in parts], axis=0).astype(BF16) for v in range(3)]
        for half in range(2):
            got = jnp.dot(
                jnp.concatenate([tiles[half], tiles[half + 1]], axis=1), weights[half],
                preferred_element_type=F32,
            ).astype(BF16).astype(F32)
            for i, (ts, z, hop) in enumerate(users):
                img[ts * 2 + z, hop, :, LANES * half:LANES * (half + 1)] = got[GROUPS * i:GROUPS * (i + 1)]

    def local(z):
        def one(t, carry):
            for x2 in range(LY):
                here = block_weights(pack_x[z, t, x2])
                beside = block_weights(pack_x[1 - z, t, x2])
                for x1 in range(LX):
                    s = x1 * LY + x2
                    users = (
                        (t * SITES + s, z, 0),
                        ((1 - t) * SITES + s, z, 2 - t),
                        (t * SITES + (1 - x1) * LY + x2, z, 5 if x1 == 1 else 6),
                        (t * SITES + x1 * LY + (x2 + 2) % LY, z, 7),
                        (t * SITES + x1 * LY + (x2 + 1) % LY, z, 8),
                    )
                    images(users, here[x1])
                    images(((t * SITES + s, z, 3 + z),), beside[x1])
            return carry

        lax.fori_loop(0, 2, one, 0, unroll=True)

    column = lax.broadcasted_iota(jnp.int32, (1, SITES * GROUPS), 1)
    agg_load.wait()
    member = [agg_ref[s].astype(F32) for s in range(SITES)]
    others = [1.0 - m for m in member]
    weight_of = (others, member)
    mask = []
    for a in range(AGGS):
        row = jnp.zeros((1, SITES * GROUPS), F32)
        for s in range(SITES):
            inside = jnp.logical_and(column >= s * GROUPS, column < (s + 1) * GROUPS)
            row = row + jnp.where(inside, weight_of[a][s], 0.0)
        mask.append(row)
    pad = jnp.zeros((2 * LANES - SITES * GROUPS, LANES), F32)

    def left_side(t, z):
        tz = t * 2 + z
        for h in range(2):
            blocks = [vec_f[t * SITES + s, pl.ds(2 * h + z, GROUPS, stride=4), :] for s in range(SITES)]
            spare = t * 2 + h
            turned = jnp.transpose(jnp.concatenate(blocks + [pad], axis=0))
            for side in range(2):
                turn[spare, side] = turned[:, LANES * side:LANES * (side + 1)]
            for low in range(2):
                for par in range(2):
                    rows = jnp.concatenate(
                        [turn[spare, side, pl.ds(low * NULLCOLS + par, 32, stride=2), :] for side in range(2)],
                        axis=1,
                    )[:, :SITES * GROUPS]
                    for a in range(AGGS):
                        at = ((a * 2 + low) * 2 + par) * 32
                        left[tz, h, at:at + 32, :] = (rows * mask[a]).astype(BF16)

    def t_side(t, z):
        def one(x2, carry):
            both = block_weights(halo_t[t, z, x2])
            for x1 in range(LX):
                images(((t * SITES + x1 * LY + x2, z, 2 - t),), both[x1])
            return carry

        lax.fori_loop(0, LY, one, 0, unroll=True)

    def z_side(t, z):
        def one(x2, carry):
            both = block_weights(halo_z[z, t, x2])
            for x1 in range(LX):
                images(((t * SITES + x1 * LY + x2, z, 4 - z),), both[x1])
            return carry

        lax.fori_loop(0, LY, one, 0, unroll=True)

    def x_side(z):
        def one(s, carry):
            x1, x2 = s // LY, s % LY
            both = block_weights(halo_x[x1, z, x2])
            for t in range(2):
                images(((t * SITES + s, z, 6 - x1),), both[t])
            return carry

        lax.fori_loop(0, SITES, one, 0, unroll=True)

    low32 = lane_half(32)

    def product(t, z, n, keep):
        tz = t * 2 + z
        t_stay, t_leave = (1, 2) if t == 1 else (2, 1)
        z_stay, z_leave = (3, 4) if z == 1 else (4, 3)
        right = []
        for h in range(2):
            cut = slice(LANES * h, LANES * (h + 1))
            columns = [[], []]
            blank = jnp.zeros((GROUPS, LANES), F32)
            for s in range(SITES):
                x1, x2 = s // LY, s % LY
                at = (t * SITES + s) * 2 + z
                take = lambda hop: img[at, hop, :, cut]
                x_stay, x_leave = (6, 5) if x1 == 1 else (5, 6)
                across = (1 - x1) * LY + x2
                up, down = x1 * LY + (x2 + 1) % LY, x1 * LY + (x2 + 2) % LY
                if n == 0:
                    same = take(0) + take(t_stay) + take(z_stay)
                    inner, plus, minus = take(x_stay), take(7), take(8)
                    for b in range(AGGS):
                        w = weight_of[b]
                        columns[b].append(w[s] * same + w[across] * inner + w[up] * plus + w[down] * minus)
                elif n == 3:
                    columns[0].append(take(t_leave))
                    columns[1].append(take(z_leave))
                else:
                    outer = take(x_leave) if x1 == 2 - n else None
                    for b in range(AGGS):
                        columns[b].append(blank if outer is None else weight_of[b][across] * outer)
            right.append(
                jnp.concatenate([jnp.concatenate(c, axis=0).astype(BF16) for c in columns], axis=1)
            )
        for a in range(AGGS):
            rows = slice(LANES * a, LANES * (a + 1))
            got = jnp.dot(left[tz, 0, rows, :], right[0], preferred_element_type=F32)
            got = got + jnp.dot(left[tz, 1, rows, :], right[1], preferred_element_type=F32)
            for c in range(2):
                cut = got[:, LANES * c:LANES * (c + 1)]
                value = jnp.where(low32, cut[0:32] + swap(cut[64:96]), swap(cut[32:64]) + cut[96:128])
                keep(n * 4 + a * 2 + c if n < 3 else 12 + c * 2 + a, value)

    def to_send(z):
        def keep(block, value):
            pt_out[z, block] = value.astype(BF16)

        return keep

    def to_keep(z):
        def keep(block, value):
            part[z, block] = value

        return keep

    left_side(1, 1)
    left_side(0, 1)
    local(1)
    product(1, 1, 3, to_send(1))
    pt[1, 2].start()
    product(0, 1, 3, to_keep(1))
    for face in x_face[1]:
        face.wait_recv()
    x_side(1)
    for n in (1, 2):
        product(1, 1, n, to_send(1))
    pt[1, 1].start()
    for n in (1, 2):
        product(0, 1, n, to_keep(1))
    pt[1, 2].wait_recv()
    for a in range(AGGS):
        pz_out[12 + a] = part[1, 12 + a].astype(BF16)
        pz_out[14 + a] = pt_in[1, 12 + a]
        pz_out[16 + a] = (part[1, 14 + a] + pt_in[1, 14 + a].astype(F32)).astype(BF16)
    pz[2].start()
    for face in t_face[1]:
        face.wait_recv()
    t_side(1, 1)
    z_face[1].wait_recv()
    z_side(1, 1)
    product(1, 1, 0, to_send(1))
    pt[1, 0].start()
    t_side(0, 1)
    z_side(0, 1)
    product(0, 1, 0, to_keep(1))
    pt[1, 1].wait_recv()
    for block in range(4, 12):
        pz_out[block] = (part[1, block] + pt_in[1, block].astype(F32)).astype(BF16)
    pz[1].start()
    pt[1, 0].wait_recv()
    for block in range(4):
        pz_out[block] = (part[1, block] + pt_in[1, block].astype(F32)).astype(BF16)
    pz[0].start()

    left_side(1, 0)
    left_side(0, 0)
    local(0)
    product(1, 0, 3, to_send(0))
    product(0, 0, 3, to_keep(0))
    for face in x_face[0]:
        face.wait_recv()
    x_side(0)
    for n in (1, 2):
        product(1, 0, n, to_send(0))
    pt[0, 1].start()
    for n in (1, 2):
        product(0, 0, n, to_keep(0))
    for face in t_face[0]:
        face.wait_recv()
    t_side(1, 0)
    t_side(0, 0)
    z_face[0].wait_recv()
    z_side(1, 0)
    product(1, 0, 0, to_send(0))
    pt[0, 0].start()
    z_side(0, 0)
    product(0, 0, 0, to_keep(0))
    pt[0, 1].wait_recv()
    for block in (*range(4, 12), 14, 15):
        part[0, block] = part[0, block] + pt_in[0, block].astype(F32)
    pz[2].wait_recv()
    for a in range(AGGS):
        cross_ref[0, pl.ds(a, 32, stride=2), :] = part[0, 12 + a] + pz_in[12 + a].astype(F32)
        cross_ref[1, pl.ds(a, 32, stride=2), :] = pt_in[0, 12 + a].astype(F32) + pz_in[14 + a].astype(F32)
        cross_ref[2, pl.ds(a, 32, stride=2), :] = part[0, 14 + a]
        cross_ref[3, pl.ds(a, 32, stride=2), :] = pz_in[16 + a].astype(F32)

    def finish(blocks):
        for block in blocks:
            within_ref[block // 2, pl.ds(block % 2, 32, stride=2), :] = part[0, block] + pz_in[block].astype(F32)

    pz[1].wait_recv()
    finish(range(4, 12))
    pt[0, 0].wait_recv()
    for block in range(4):
        part[0, block] = part[0, block] + pt_in[0, block].astype(F32)
    pz[0].wait_recv()
    finish(range(4))
    for copy in (*x_face[0], *x_face[1], *t_face[0], *t_face[1], *z_face, *pt.values(), *pz):
        copy.wait_send()


def lane_tiles(field):
    time, depth, sites, length = field.shape
    split = field.reshape(time, depth, sites, length // LANES, LANES)
    return split.transpose(0, 2, 3, 1, 4).reshape(time, sites, length // LANES * depth, LANES)


def per_device(operator, vectors, aggregate):
    op_rows = HOPS * BLOCK * BLOCK // LANES * 2
    vec_rows = BLOCK * NULLCOLS // LANES * 2
    within, cross = pl.pallas_call(
        kernel,
        out_shape=(
            jax.ShapeDtypeStruct((3 * AGGS, 64, LANES), F32),
            jax.ShapeDtypeStruct((4, 64, LANES), F32),
        ),
        in_specs=[
            pl.BlockSpec(memory_space=pltpu.HBM),
            pl.BlockSpec(memory_space=pltpu.HBM),
            pl.BlockSpec(memory_space=pltpu.HBM),
        ],
        out_specs=[pl.BlockSpec(memory_space=pltpu.VMEM)] * 2,
        scratch_shapes=[
            pltpu.SMEM((SITES,), jnp.int32),
            pltpu.VMEM((2, SITES, op_rows, LANES), BF16),
            pltpu.VMEM((2, SITES, vec_rows, LANES), BF16),
            pltpu.VMEM((2 * SITES, op_rows, LANES), F32),
            pltpu.VMEM((2 * SITES, vec_rows, LANES), F32),
            pltpu.VMEM((4, BLOCK, LANES), F32),
            pltpu.VMEM((2, SITES, BLOCK, LANES), BF16),
            pltpu.VMEM((2, 2, LY, BLOCK, LANES), BF16),
            pltpu.VMEM((2, 2, LY, BLOCK, LANES), BF16),
            pltpu.VMEM((2, 2, LY, BLOCK, LANES), BF16),
            pltpu.VMEM((2, 2, LY, BLOCK, LANES), BF16),
            pltpu.VMEM((4 * SITES, HOPS, GROUPS, 2 * LANES), F32),
            pltpu.VMEM((4, 2, LANES, LANES), F32),
            pltpu.VMEM((4, 2, 2 * LANES, SITES * GROUPS), BF16),
            pltpu.VMEM((2, 16, 32, LANES), F32),
            pltpu.VMEM((2, 16, 32, LANES), BF16),
            pltpu.VMEM((2, 16, 32, LANES), BF16),
            pltpu.VMEM((18, 32, LANES), BF16),
            pltpu.VMEM((18, 32, LANES), BF16),
            pltpu.SemaphoreType.DMA((4,)),
            pltpu.SemaphoreType.DMA((18,)),
            pltpu.SemaphoreType.DMA((18,)),
        ],
        compiler_params=pltpu.CompilerParams(
            collective_id=0, has_side_effects=True, vmem_limit_bytes=40 << 20
        ),
    )(
        pltpu.with_memory_space_constraint(aggregate, pltpu.HBM),
        pltpu.with_memory_space_constraint(lane_tiles(operator), pltpu.HBM),
        pltpu.with_memory_space_constraint(lane_tiles(vectors), pltpu.HBM),
    )
    within = within.reshape(3, AGGS, 32, AGGS, LANES).transpose(0, 1, 3, 2, 4)
    cross = cross.reshape(4, 32, AGGS, LANES).transpose(0, 2, 1, 3)
    return (
        within.reshape(1, 1, 3, AGGS, AGGS, NULLCOLS * NULLCOLS),
        cross.reshape(1, 1, 4, AGGS, NULLCOLS * NULLCOLS),
    )


def solution(mesh):
    return jax.shard_map(
        per_device,
        mesh=mesh,
        in_specs=(P("ta", "sa", None, None), P("ta", "sa", None, None), P()),
        out_specs=(P("ta", "sa", None, None, None, None), P("ta", "sa", None, None, None)),
        check_vma=False,
    )
```
